32 devices in a mesh: orb: 8 (over y, x, core), aux: 4 (over z).
Axes of the slice: x: 2, y: 2, z: 4, core: 2. Of those that a mesh axis runs over, the one named last changes fastest.
Arguments:
- orbital_slabs: float32 [8, 8192, 1024], P('orb', 'aux'), may hold values from -0.625 to 0.625
- occupied_energy: float32 [8], replicated, may hold values from -1.5 to -0.3
- virtual_energy: float32 [1024], replicated, may hold values from 0.3 to 2.5
- virtual_count: int32 [8], replicated, may hold values from 512 to 1024, as said below
Outputs:
- density: float32 [8, 8192, 1024], P('orb', 'aux')
The draws below stay inside these ranges and needn't reach their ends.
Inputs may be any that keep to these rules, and one draw needn't show every extreme that they name: `virtual_count`: the largest count is 1024 in every draw.
All inputs are finite; a program needn't handle non-finite values.
Results may differ from the reference program's by a relative error of at most 0.0003.
Values sent between devices are 32-bit elements; how exact they have to be, the bound alone decides.
A program may use at most 64 MiB of HBM per device.

```python
import jax
import jax.numpy as jnp
from jax import lax

NV = 1024
NAUX = 8192
ROUNDS = 1
NOCC = 8


def draw_virtual_count(key, part):
    key_counts, key_pick = jax.random.split(key)
    counts = jax.random.randint(key_counts, (NOCC,), NV // 2, NV + 1)
    picked = jax.random.randint(key_pick, (), 0, NOCC)
    return jnp.where(jnp.arange(NOCC) == picked, NV, counts).astype(jnp.int32)


def block_levels(key, shape, pieces, least, top_value):
    level = 1.0
    for dim, shards_of in pieces:
        draws = jax.random.uniform(jax.random.fold_in(jax.random.fold_in(key, 6), dim), (shards_of,), jnp.float32, least / len(pieces), top_value / len(pieces))
        level = level * jnp.repeat(jnp.exp(draws), shape[dim] // shards_of).reshape((-1,) + (1,) * (len(shape) - 1 - dim))
    return level


def bell_draw(rng, dims, spread, reach, cuts=(), kind=jnp.bfloat16):
    values = jax.random.normal(rng, dims, jnp.float32) * spread
    if len(cuts) > 0:
        values = block_levels(rng, dims, cuts, -0.22, 0.18) * values
    return jnp.clip(values, min=-reach, max=reach).astype(kind)


def setup_inputs(seed: int = 0) -> dict:
    streams_of = jax.random.split(jax.random.key(seed), 5)
    return {
        "orbital_slabs": bell_draw(streams_of[0], (NOCC, NAUX, NV), (NAUX ** 0.5) ** -0.5, 0.625, ((0, 8), (1, 4)), jnp.float32),
        "occupied_energy": jnp.clip(jax.random.uniform(streams_of[1], (NOCC,), jnp.float32, -1.5, -0.3), -1.5, -0.3),
        "virtual_energy": jnp.clip(jax.random.uniform(streams_of[2], (NV,), jnp.float32, 0.3, 2.5), 0.3, 2.5),
        "virtual_count": draw_virtual_count(jax.random.fold_in(streams_of[4], 71), 0),
    }


highest_mode = lax.Precision.HIGHEST


def amplitudes(coupling, occupied_energy, virtual_energy, virtual_count, orbital_one, orbital_two):
    positions = jnp.arange(virtual_energy.shape[0], dtype=jnp.int32)
    mask_one = (positions < virtual_count[orbital_one]).astype(jnp.float32)
    mask_two = (positions < virtual_count[orbital_two]).astype(jnp.float32)
    denominator = virtual_energy[:, None] + virtual_energy[None, :] - occupied_energy[orbital_one] - occupied_energy[orbital_two]
    return (2.0 * coupling - coupling.T) * mask_one[:, None] * mask_two[None, :] / denominator


def reference(orbital_slabs, occupied_energy, virtual_energy, virtual_count):
    orbitals = orbital_slabs.shape[0]
    density = jnp.zeros(orbital_slabs.shape, jnp.float32)
    for distance in range(1, ROUNDS + 1):
        def advance(density, orbital_one):
            orbital_two = ((orbital_one + distance) % orbitals).astype(jnp.int32)
            slab_one = lax.dynamic_index_in_dim(orbital_slabs, orbital_one, 0, keepdims=False)
            slab_two = lax.dynamic_index_in_dim(orbital_slabs, orbital_two, 0, keepdims=False)
            coupling = lax.dot_general(slab_one, slab_two, (((0,), (0,)), ((), ())), precision=highest_mode, preferred_element_type=jnp.float32)
            amplitude = amplitudes(coupling, occupied_energy, virtual_energy, virtual_count, orbital_one, orbital_two)
            term_one = lax.dot_general(slab_two, amplitude, (((1,), (1,)), ((), ())), precision=highest_mode, preferred_element_type=jnp.float32)
            term_two = jnp.dot(slab_one, amplitude, precision=highest_mode, preferred_element_type=jnp.float32)
            density = density.at[orbital_one].add(term_one)
            density = density.at[orbital_two].add(term_two)
            return density, None

        density, unused = lax.scan(advance, density, jnp.arange(orbitals, dtype=jnp.int32))
    return density
```

```python
import functools

import jax
import jax.numpy as jnp
from jax import lax
from jax.experimental import pallas as pl
from jax.experimental.pallas import tpu as pltpu
from jax.sharding import PartitionSpec as P

MESH = pl.DeviceIdType.MESH
NN = (((1,), (0,)), ((), ()))
NT = (((1,), (1,)), ((), ()))


def halves(x):
    high = x.astype(jnp.bfloat16)
    return high, (x - high.astype(jnp.float32)).astype(jnp.bfloat16)


def dot3(ah, al, bh, bl, dims):
    dot = functools.partial(lax.dot_general, dimension_numbers=dims, preferred_element_type=jnp.float32)
    return dot(ah, bh) + (dot(ah, bl) + dot(al, bh))


def pair_kernel(
    orbs, auxs, chunk, block,
    slab_hbm, mask_one, virt_col, mask_two, virt_row,
    near_hbm, far_hbm,
    own, high, low, partner, part_high, part_low, coupling, prefix, suffix, send_up,
    amp_high, amp_low,
    load_sem, slab_send, slab_recv, right_send, right_recv, left_send, left_recv,
    far_send, far_recv, near_sem,
):
    rows, virtuals = own.shape
    chunks, blocks = virtuals // chunk, rows // block
    o, z = lax.axis_index("orb"), lax.axis_index("aux")
    before, after = lax.rem(o + orbs - 1, orbs), lax.rem(o + 1, orbs)
    first, last = z == 0, z == auxs - 1

    load = pltpu.make_async_copy(slab_hbm, own, load_sem)
    load.start()

    barrier = pltpu.get_barrier_semaphore()
    for there in (before, after):
        pl.semaphore_signal(barrier, inc=1, device_id=(there, z), device_id_type=MESH)

    @pl.when(z > 0)
    def _():
        pl.semaphore_signal(barrier, inc=1, device_id=(o, z - 1), device_id_type=MESH)

    @pl.when(z < auxs - 1)
    def _():
        pl.semaphore_signal(barrier, inc=1, device_id=(o, z + 1), device_id_type=MESH)

    ends = jnp.where(first, 1, 0) + jnp.where(last, 1, 0)
    pl.semaphore_wait(barrier, 4 - ends)

    def slab_copy(c):
        columns = pl.ds(pl.multiple_of(c * chunk, chunk), chunk)
        return pltpu.make_async_remote_copy(
            src_ref=slab_hbm.at[:, columns], dst_ref=partner.at[:, columns],
            send_sem=slab_send.at[c], recv_sem=slab_recv.at[c],
            device_id=(before, z), device_id_type=MESH)

    def right_copy(k):
        return pltpu.make_async_remote_copy(
            src_ref=prefix.at[k], dst_ref=prefix.at[k],
            send_sem=right_send.at[k], recv_sem=right_recv.at[k],
            device_id=(o, lax.rem(z + 1, auxs)), device_id_type=MESH)

    def left_copy(k):
        return pltpu.make_async_remote_copy(
            src_ref=send_up.at[k], dst_ref=suffix.at[k],
            send_sem=left_send.at[k], recv_sem=left_recv.at[k],
            device_id=(o, lax.rem(z + auxs - 1, auxs)), device_id_type=MESH)

    def far_copy(r):
        span = pl.ds(pl.multiple_of(r * block, block), block)
        return pltpu.make_async_remote_copy(
            src_ref=own.at[span], dst_ref=far_hbm.at[span],
            send_sem=far_send.at[r], recv_sem=far_recv.at[r],
            device_id=(after, z), device_id_type=MESH)

    def near_copy(r):
        span = pl.ds(pl.multiple_of(r * block, block), block)
        return pltpu.make_async_copy(partner.at[span], near_hbm.at[span], near_sem.at[r])

    def each(count, body):
        lax.fori_loop(0, count, lambda i, x: (body(i), x)[1], 0)

    each(chunks, lambda c: slab_copy(c).start())

    @pl.when(first)
    def _():
        prefix[...] = jnp.zeros_like(prefix)

    @pl.when(last)
    def _():
        suffix[...] = jnp.zeros_like(suffix)

    load.wait()

    def split_own(r):
        span = pl.ds(pl.multiple_of(r * block, block), block)
        high[span], low[span] = halves(own[span])

    each(blocks, split_own)

    def couple(c):
        slab_copy(c).wait_recv()
        columns = pl.ds(pl.multiple_of(c * chunk, chunk), chunk)

        def turn(r):
            span = pl.ds(pl.multiple_of(r * block, block), block)
            part_high[:, span], part_low[:, span] = halves(partner[span, columns].T)

        each(blocks, turn)

        def tile(t):
            width = pl.ds(pl.multiple_of(t * block, block), block)
            coupling[c, :, width] = dot3(part_high[...], part_low[...], high[:, width], low[:, width], NN)

        each(virtuals // block, tile)

    def step(s):
        @pl.when(s < chunks)
        def _():
            couple(s)

        k = s - z

        @pl.when((k >= 0) & (k < chunks))
        def _():
            @pl.when(z > 0)
            def _():
                right_copy(k).wait_recv()

            prefix[k] = prefix[k] + coupling[k]

            @pl.when(z < auxs - 1)
            def _():
                right_copy(k).start()

        m = s - (auxs - 1 - z)

        @pl.when((m >= 0) & (m < chunks))
        def _():
            @pl.when(z < auxs - 1)
            def _():
                left_copy(m).wait_recv()

            send_up[m] = suffix[m] + coupling[m]

            @pl.when(z > 0)
            def _():
                left_copy(m).start()

    each(chunks + auxs - 1, step)

    @pl.when(z < auxs - 1)
    def _():
        each(chunks, lambda k: right_copy(k).wait_send())

    @pl.when(z > 0)
    def _():
        each(chunks, lambda k: left_copy(k).wait_send())

    def total(k):
        coupling[k] = prefix[k] + suffix[k]

    each(chunks, total)

    def amplitude(k):
        span = pl.ds(pl.multiple_of(k * chunk, chunk), chunk)
        for m in range(chunks):
            columns = pl.ds(m * chunk, chunk)
            straight = coupling[m, :, span].T
            crossed = coupling[k, :, columns]
            value = (2.0 * straight - crossed) * mask_one[span] * mask_two[:, columns]
            value = value / (virt_col[span] + virt_row[:, columns])
            amp_high[span, columns], amp_low[span, columns] = halves(value)

    each(chunks, amplitude)

    def far_term(r):
        span = pl.ds(pl.multiple_of(r * block, block), block)

        def tile(t):
            width = pl.ds(pl.multiple_of(t * block, block), block)
            own[span, width] = dot3(high[span], low[span], amp_high[:, width], amp_low[:, width], NN)

        each(virtuals // block, tile)
        far_copy(r).start()

    each(blocks, far_term)

    def near_term(r):
        span = pl.ds(pl.multiple_of(r * block, block), block)
        part_high_r, part_low_r = halves(partner[span])

        def tile(t):
            width = pl.ds(pl.multiple_of(t * block, block), block)
            own_rows = dot3(part_high_r, part_low_r, amp_high[width], amp_low[width], NT)
            partner[span, width] = own_rows

        each(virtuals // block, tile)
        near_copy(r).start()

    each(blocks, near_term)
    each(chunks, lambda c: slab_copy(c).wait_send())
    each(blocks, lambda r: near_copy(r).wait())
    each(blocks, lambda r: far_copy(r).wait())


def shards(orbital_slabs, occupied_energy, virtual_energy, virtual_count):
    slab = orbital_slabs[0]
    rows, virtuals = slab.shape
    orbs, auxs = lax.axis_size("orb"), lax.axis_size("aux")
    o = lax.axis_index("orb")
    j = (o + 1) % orbs
    positions = jnp.arange(virtuals, dtype=jnp.int32)
    mask_one = (positions < virtual_count[o]).astype(jnp.float32)[:, None]
    mask_two = (positions < virtual_count[j]).astype(jnp.float32)[None, :]
    virt_row = (virtual_energy - (occupied_energy[o] + occupied_energy[j]))[None, :]
    chunk = min(128, virtuals)
    block = min(256, rows)
    chunks, blocks = virtuals // chunk, rows // block
    vmem = pl.BlockSpec(memory_space=pltpu.VMEM)
    hbm = pl.BlockSpec(memory_space=pl.ANY)
    f32, bf16 = jnp.float32, jnp.bfloat16
    dma = pltpu.SemaphoreType.DMA
    near, far = pl.pallas_call(
        functools.partial(pair_kernel, orbs, auxs, chunk, block),
        out_shape=[jax.ShapeDtypeStruct((rows, virtuals), f32)] * 2,
        in_specs=[hbm, vmem, vmem, vmem, vmem],
        out_specs=[hbm, hbm],
        scratch_shapes=[
            pltpu.VMEM((rows, virtuals), f32),
            pltpu.VMEM((rows, virtuals), bf16),
            pltpu.VMEM((rows, virtuals), bf16),
            pltpu.VMEM((rows, virtuals), f32),
            pltpu.VMEM((chunk, rows), bf16),
            pltpu.VMEM((chunk, rows), bf16),
            pltpu.VMEM((chunks, chunk, virtuals), f32),
            pltpu.VMEM((chunks, chunk, virtuals), f32),
            pltpu.VMEM((chunks, chunk, virtuals), f32),
            pltpu.VMEM((chunks, chunk, virtuals), f32),
            pltpu.VMEM((virtuals, virtuals), bf16),
            pltpu.VMEM((virtuals, virtuals), bf16),
            dma, dma((chunks,)), dma((chunks,)), dma((chunks,)), dma((chunks,)),
            dma((chunks,)), dma((chunks,)), dma((blocks,)), dma((blocks,)), dma((blocks,)),
        ],
        cost_estimate=pl.CostEstimate(
            flops=18 * rows * virtuals * virtuals, bytes_accessed=16 * rows * virtuals, transcendentals=0),
        compiler_params=pltpu.CompilerParams(
            collective_id=0, has_side_effects=True, vmem_limit_bytes=58 * 2**20),
    )(slab, mask_one, virtual_energy[:, None], mask_two, virt_row)
    return (near + far)[None]


def solution(mesh):
    placed = (P("orb", "aux", None), P(), P(), P())
    return jax.shard_map(
        shards, mesh=mesh, in_specs=placed, out_specs=P("orb", "aux", None), check_vma=False
    )
```

```python
import functools

import jax
import jax.numpy as jnp
from jax import lax
from jax.experimental import pallas as pl
from jax.experimental.pallas import tpu as pltpu
from jax.sharding import PartitionSpec as P

MESH = pl.DeviceIdType.MESH
NN = (((1,), (0,)), ((), ()))
NT = (((1,), (1,)), ((), ()))


def halves(x):
    high = x.astype(jnp.bfloat16)
    return high, (x - high.astype(jnp.float32)).astype(jnp.bfloat16)


def dot3(ah, al, bh, bl, dims):
    dot = functools.partial(lax.dot_general, dimension_numbers=dims, preferred_element_type=jnp.float32)
    return dot(ah, bh) + (dot(ah, bl) + dot(al, bh))


def pair_kernel(
    orbs, auxs, chunk, block, strip, piece, ahead,
    slab_hbm, occupied, counts, virt_row,
    near_hbm, far_hbm,
    own, high, low, partner, part_high, part_low, coupling, prefix, suffix, send_up,
    amp_high, amp_low,
    load_sem, slab_send, slab_recv, right_send, right_recv, left_send, left_recv,
    far_send, far_recv, near_sem,
):
    rows, virtuals = own.shape
    chunks, blocks = virtuals // chunk, rows // block
    o, z = lax.axis_index("orb"), lax.axis_index("aux")
    before, after = lax.rem(o + orbs - 1, orbs), lax.rem(o + 1, orbs)
    first, last = z == 0, z == auxs - 1

    load = pltpu.make_async_copy(slab_hbm, own, load_sem)
    load.start()

    barrier = pltpu.get_barrier_semaphore()
    for there in (before, after):
        pl.semaphore_signal(barrier, inc=1, device_id=(there, z), device_id_type=MESH)

    @pl.when(z > 0)
    def _():
        pl.semaphore_signal(barrier, inc=1, device_id=(o, z - 1), device_id_type=MESH)

    @pl.when(z < auxs - 1)
    def _():
        pl.semaphore_signal(barrier, inc=1, device_id=(o, z + 1), device_id_type=MESH)

    ends = jnp.where(first, 1, 0) + jnp.where(last, 1, 0)
    pl.semaphore_wait(barrier, 4 - ends)

    def slab_copy(c):
        columns = pl.ds(pl.multiple_of(c * chunk, chunk), chunk)
        return pltpu.make_async_remote_copy(
            src_ref=slab_hbm.at[:, columns], dst_ref=partner.at[:, columns],
            send_sem=slab_send.at[c], recv_sem=slab_recv.at[c],
            device_id=(before, z), device_id_type=MESH)

    def piece_of(k):
        return pl.ds(pl.multiple_of(k * piece, piece), piece)

    def right_copy(k):
        return pltpu.make_async_remote_copy(
            src_ref=prefix.at[piece_of(k)], dst_ref=prefix.at[piece_of(k)],
            send_sem=right_send.at[k], recv_sem=right_recv.at[k],
            device_id=(o, lax.rem(z + 1, auxs)), device_id_type=MESH)

    def left_copy(k):
        return pltpu.make_async_remote_copy(
            src_ref=send_up.at[piece_of(k)], dst_ref=suffix.at[piece_of(k)],
            send_sem=left_send.at[k], recv_sem=left_recv.at[k],
            device_id=(o, lax.rem(z + auxs - 1, auxs)), device_id_type=MESH)

    def far_copy(r):
        span = pl.ds(pl.multiple_of(r * strip, strip), strip)
        return pltpu.make_async_remote_copy(
            src_ref=own.at[span], dst_ref=far_hbm.at[span],
            send_sem=far_send.at[r], recv_sem=far_recv.at[r],
            device_id=(after, z), device_id_type=MESH)

    def near_copy(r):
        span = pl.ds(pl.multiple_of(r * block, block), block)
        return pltpu.make_async_copy(partner.at[span], near_hbm.at[span], near_sem.at[r])

    def each(count, body):
        lax.fori_loop(0, count, lambda i, x: (body(i), x)[1], 0)

    each(ahead, lambda c: slab_copy(c).start())

    @pl.when(first)
    def _():
        prefix[...] = jnp.zeros_like(prefix)

    @pl.when(last)
    def _():
        suffix[...] = jnp.zeros_like(suffix)

    load.wait()

    def split_own(r):
        span = pl.ds(pl.multiple_of(r * block, block), block)
        high[span], low[span] = halves(own[span])

    each(blocks, split_own)

    def couple(c):
        slab_copy(c).wait_recv()
        columns = pl.ds(pl.multiple_of(c * chunk, chunk), chunk)

        def turn(r):
            span = pl.ds(pl.multiple_of(r * block, block), block)
            part_high[:, span], part_low[:, span] = halves(partner[span, columns].T)

        each(blocks, turn)

        def tile(t):
            width = pl.ds(pl.multiple_of(t * block, block), block)
            coupling[columns, width] = dot3(part_high[...], part_low[...], high[:, width], low[:, width], NN)

        each(virtuals // block, tile)

    count_one, count_two = counts[o], counts[lax.rem(o + 1, orbs)]
    pair_energy = occupied[o] + occupied[lax.rem(o + 1, orbs)]
    square = (chunk, chunk)
    down = lax.broadcasted_iota(jnp.int32, square, 0)
    along = lax.broadcasted_iota(jnp.int32, square, 1)

    def amplitude(k):
        held = pl.ds(pl.multiple_of(k * chunk, chunk), chunk)
        coupling[held] = prefix[held] + suffix[held]
        energy_k = jnp.broadcast_to(virt_row[:, held], square)

        def pair(m):
            other = pl.ds(pl.multiple_of(m * chunk, chunk), chunk)
            gap = energy_k.T + virt_row[:, other] - pair_energy
            at_k, at_m = coupling[held, other], coupling[other, held]
            value = (2.0 * at_m.T - at_k) / gap
            keep = (down + k * chunk < count_one) & (along + m * chunk < count_two)
            amp_high[held, other], amp_low[held, other] = halves(jnp.where(keep, value, 0.0))
            value = (2.0 * at_k.T - at_m) / gap.T
            keep = (down + m * chunk < count_one) & (along + k * chunk < count_two)
            amp_high[other, held], amp_low[other, held] = halves(jnp.where(keep, value, 0.0))

        each(k + 1, pair)

    def right_step(k):
        @pl.when(z > 0)
        def _():
            right_copy(k).wait_recv()

        prefix[piece_of(k)] = prefix[piece_of(k)] + coupling[piece_of(k)]

        @pl.when(z < auxs - 1)
        def _():
            right_copy(k).start()

    def left_step(k):
        @pl.when(z < auxs - 1)
        def _():
            left_copy(k).wait_recv()

        send_up[piece_of(k)] = suffix[piece_of(k)] + coupling[piece_of(k)]

        @pl.when(z > 0)
        def _():
            left_copy(k).start()

    split = chunk // piece

    def step(s):
        @pl.when(s < chunks)
        def _():
            couple(s)

        if ahead < chunks:
            @pl.when(s + ahead < chunks)
            def _():
                slab_copy(s).wait_send()
                slab_copy(s + ahead).start()

        k = s - (z + 1) // 2

        @pl.when((k >= 0) & (k < chunks))
        def _():
            each(split, lambda p: right_step(k * split + p))

        m = s - (auxs - z) // 2

        @pl.when((m >= 0) & (m < chunks))
        def _():
            each(split, lambda p: left_step(m * split + p))

        @pl.when(s >= auxs // 2)
        def _():
            amplitude(s - auxs // 2)

    each(chunks + auxs // 2, step)

    def far_term(r):
        span = pl.ds(pl.multiple_of(r * strip, strip), strip)

        def tile(t):
            width = pl.ds(pl.multiple_of(t * block, block), block)
            own[span, width] = dot3(high[span], low[span], amp_high[:, width], amp_low[:, width], NN)

        each(virtuals // block, tile)
        far_copy(r).start()

    each(rows // strip, far_term)

    def near_term(r):
        span = pl.ds(pl.multiple_of(r * block, block), block)
        part_high_r, part_low_r = halves(partner[span])

        def tile(t):
            width = pl.ds(pl.multiple_of(t * block, block), block)
            own_rows = dot3(part_high_r, part_low_r, amp_high[width], amp_low[width], NT)
            partner[span, width] = own_rows

        each(virtuals // block, tile)
        near_copy(r).start()

    each(blocks, near_term)
    each(ahead, lambda c: slab_copy(chunks - ahead + c).wait_send())

    @pl.when(z < auxs - 1)
    def _():
        each(chunks * split, lambda k: right_copy(k).wait_send())

    @pl.when(z > 0)
    def _():
        each(chunks * split, lambda k: left_copy(k).wait_send())

    each(blocks, lambda r: near_copy(r).wait())
    each(rows // strip, lambda r: far_copy(r).wait())


def add_kernel(near, far, total):
    total[...] = near[...] + far[...]


def chunks_ahead(chunks):
    return chunks


def shards(orbital_slabs, occupied_energy, virtual_energy, virtual_count):
    slab = orbital_slabs[0]
    rows, virtuals = slab.shape
    orbs, auxs = lax.axis_size("orb"), lax.axis_size("aux")
    chunk = min(128, virtuals)
    block = min(256, rows)
    strip = min(128, rows)
    strips = rows // strip
    piece = min(32, chunk)
    ahead = chunks_ahead(virtuals // chunk)
    pieces = virtuals // piece
    chunks, blocks = virtuals // chunk, rows // block
    vmem = pl.BlockSpec(memory_space=pltpu.VMEM)
    smem = pl.BlockSpec(memory_space=pltpu.SMEM)
    hbm = pl.BlockSpec(memory_space=pl.ANY)
    f32, bf16 = jnp.float32, jnp.bfloat16
    dma = pltpu.SemaphoreType.DMA
    near, far = pl.pallas_call(
        functools.partial(pair_kernel, orbs, auxs, chunk, block, strip, piece, ahead),
        out_shape=[jax.ShapeDtypeStruct((rows, virtuals), f32)] * 2,
        in_specs=[hbm, smem, smem, vmem],
        out_specs=[hbm, hbm],
        scratch_shapes=[
            pltpu.VMEM((rows, virtuals), f32),
            pltpu.VMEM((rows, virtuals), bf16),
            pltpu.VMEM((rows, virtuals), bf16),
            pltpu.VMEM((rows, virtuals), f32),
            pltpu.VMEM((chunk, rows), bf16),
            pltpu.VMEM((chunk, rows), bf16),
            pltpu.VMEM((virtuals, virtuals), f32),
            pltpu.VMEM((virtuals, virtuals), f32),
            pltpu.VMEM((virtuals, virtuals), f32),
            pltpu.VMEM((virtuals, virtuals), f32),
            pltpu.VMEM((virtuals, virtuals), bf16),
            pltpu.VMEM((virtuals, virtuals), bf16),
            dma, dma((chunks,)), dma((chunks,)), dma((pieces,)), dma((pieces,)),
            dma((pieces,)), dma((pieces,)), dma((strips,)), dma((strips,)), dma((blocks,)),
        ],
        cost_estimate=pl.CostEstimate(
            flops=18 * rows * virtuals * virtuals, bytes_accessed=16 * rows * virtuals, transcendentals=0),
        compiler_params=pltpu.CompilerParams(
            collective_id=0, has_side_effects=True, vmem_limit_bytes=58 * 2**20),
    )(slab, occupied_energy, virtual_count, virtual_energy[None, :])
    rows_each = pl.BlockSpec((block, virtuals), lambda r: (r, 0))
    return pl.pallas_call(
        add_kernel,
        out_shape=jax.ShapeDtypeStruct((rows, virtuals), f32),
        grid=(blocks,),
        in_specs=[rows_each, rows_each],
        out_specs=rows_each,
        cost_estimate=pl.CostEstimate(
            flops=rows * virtuals, bytes_accessed=12 * rows * virtuals, transcendentals=0),
        compiler_params=pltpu.CompilerParams(vmem_limit_bytes=32 * 2**20),
    )(near, far)[None]


def solution(mesh):
    placed = (P("orb", "aux", None), P(), P(), P())
    return jax.shard_map(
        shards, mesh=mesh, in_specs=placed, out_specs=P("orb", "aux", None), check_vma=False
    )
```
